256 devices in a mesh: acq: 16 (over z_lo, x), az: 16 (over z_hi, y, core).
Axes of the slice: x: 4, y: 4, z: 8 (z_hi: 2, z_lo: 4; z = z_hi * 4 + z_lo), core: 2. Of those that a mesh axis runs over, the one named last changes fastest.
Arguments:
- matched_images: bfloat16 [128, 2, 2048, 2048], P('acq', None, 'az'), may hold values from -6 to 6
- master_segment_duo: bfloat16 [2, 2, 2048, 2048], P(None, None, 'az', 'acq'), may hold values from -6 to 6
- along_track_whole_displacement: int32 [128, 128], P('acq', 'az'), may hold values from -1 to 0
- slant_whole_displacement: int32 [128, 128], P('acq', 'az'), may hold values from -1 to 0
- along_track_subpixel_filter: int32 [128, 128], P('acq', 'az'), may hold values from 0 to 15
- slant_subpixel_filter: int32 [128, 128], P('acq', 'az'), may hold values from 0 to 15
- tile_master_segment: int32 [128, 128], P('acq', 'az'), may hold values from 0 to 1
Outputs:
- coherence: float32 [128, 2, 512, 128], P('acq', None, 'az')
The draws below stay inside these ranges and needn't reach their ends.
All inputs are finite; a program needn't handle non-finite values.
Results may differ from the reference program's by a relative error of at most 0.0003.
Values may be sent and summed in bfloat16 or wider, within the bound.
A program may use at most 320 MiB of HBM per device.

```python
import jax
import jax.numpy as jnp
from jax import lax

SLANT_WIDTH = 2048
TAPS = 8
NFRAC = 16
TILE_HEIGHT = 16
HALO = 4
MATCHED_TOTAL = 128
ALONG_TRACK_SIZE = 2048
TILE_TOTAL = 128


def with_ends(values, own_key, least, largest):
    longest = values.shape.index(max(values.shape))
    spots = []
    for shift in (0, 1):
        where = [jax.random.randint(jax.random.fold_in(own_key, axis), (), 0, length) for axis, length in enumerate(values.shape)]
        where[longest] = (where[longest] + shift) % values.shape[longest]
        spots.append(tuple(where))
    return values.at[spots[0]].set(least).at[spots[1]].set(largest)


def level_of(stream_key, dims, shards, least, high):
    def one(axis_at, parts):
        steps = jax.random.uniform(jax.random.fold_in(jax.random.fold_in(stream_key, 6), axis_at), (parts,), jnp.float32, least / len(shards), high / len(shards))
        return jnp.repeat(jnp.exp(steps), dims[axis_at] // parts).reshape((-1,) + (1,) * (len(dims) - axis_at - 1))

    loudness = one(*shards[0])
    for cut in shards[1:]:
        loudness = loudness * one(*cut)
    return loudness


def normal_values(key, dims, width, bound, pieces=(), kind=jnp.bfloat16):
    gain = level_of(key, dims, pieces, -0.22, 0.18) if pieces else 1.0
    array = jax.random.normal(key, dims, jnp.float32) * width * gain
    return jnp.minimum(jnp.maximum(array, -bound), bound).astype(kind)


def setup_inputs(seed: int = 0) -> dict:
    keys = jax.random.split(jax.random.key(seed), 8)
    return {
        "matched_images": normal_values(keys[0], (MATCHED_TOTAL, 2, ALONG_TRACK_SIZE, SLANT_WIDTH), 1.0, 6.0, ((0, 16), (2, 16))),
        "master_segment_duo": normal_values(keys[1], (2, 2, ALONG_TRACK_SIZE, SLANT_WIDTH), 1.0, 6.0, ((2, 16), (3, 16))),
        "along_track_whole_displacement": with_ends(jax.random.randint(keys[2], (MATCHED_TOTAL, TILE_TOTAL), -1, 1), jax.random.fold_in(keys[2], 1), -1, 0).astype(jnp.int32),
        "slant_whole_displacement": with_ends(jax.random.randint(keys[3], (MATCHED_TOTAL, TILE_TOTAL), -1, 1), jax.random.fold_in(keys[3], 1), -1, 0).astype(jnp.int32),
        "along_track_subpixel_filter": with_ends(jax.random.randint(keys[4], (MATCHED_TOTAL, TILE_TOTAL), 0, NFRAC), jax.random.fold_in(keys[4], 1), 0, NFRAC - 1).astype(jnp.int32),
        "slant_subpixel_filter": with_ends(jax.random.randint(keys[5], (MATCHED_TOTAL, TILE_TOTAL), 0, NFRAC), jax.random.fold_in(keys[5], 1), 0, NFRAC - 1).astype(jnp.int32),
        "tile_master_segment": with_ends(jax.random.randint(keys[6], (MATCHED_TOTAL, TILE_TOTAL), 0, 2), jax.random.fold_in(keys[6], 1), 0, 1).astype(jnp.int32),
    }


def kernel_table():
    fraction = jnp.arange(NFRAC, dtype=jnp.float32)[:, None] / NFRAC
    distance = jnp.arange(TAPS, dtype=jnp.float32)[None, :] - 3.0 - fraction
    kernel_taps = jnp.sinc(distance) * (0.5 + 0.5 * jnp.cos(jnp.pi * distance / 4.0))
    return kernel_taps / lax.optimization_barrier(jnp.sum(kernel_taps, axis=1, keepdims=True))

def line_weights(shift, index, table):
    onehot = (index[:, None] == jnp.arange(NFRAC, dtype=jnp.int32)[None, :]).astype(jnp.float32)
    kernel_taps = lax.optimization_barrier(jnp.sum(onehot[:, :, None] * table[None, :, :], axis=1))
    placed = jnp.arange(TAPS + 1, dtype=jnp.int32)[None, None, :] == 1 + jnp.arange(TAPS, dtype=jnp.int32)[None, :, None] + shift[:, None, None]
    weights = lax.optimization_barrier(jnp.sum(kernel_taps[:, :, None] * placed.astype(jnp.float32), axis=1))
    return jnp.repeat(weights, TILE_HEIGHT, axis=0)

def resample(padded, az_weight, rg_weight):
    line_count = az_weight.shape[0]
    summed = az_weight[None, :, 0, None] * padded[:, 0:line_count, :]
    for tap in range(1, TAPS + 1):
        summed = summed + az_weight[None, :, tap, None] * padded[:, tap:tap + line_count, :]
    columns = summed.shape[2]
    widened = jnp.pad(summed, ((0, 0), (0, 0), (4, 4)))
    result = rg_weight[None, :, 0, None] * widened[:, :, 0:columns]
    for tap in range(1, TAPS + 1):
        result = result + rg_weight[None, :, tap, None] * widened[:, :, tap:tap + columns]
    return result

def looks(values):
    lead = values.shape[:-2]
    line_count = values.shape[-2]
    columns = values.shape[-1]
    shaped = values.reshape(lead + (line_count // 4, 4, columns // 16, 16))
    return lax.optimization_barrier(jnp.sum(shaped, axis=(-3, -1)))

def correlation_magnitude(coregistered, chosen_master_segment):
    real_s = coregistered[..., 0, :, :]
    imag_s = coregistered[..., 1, :, :]
    master_inphase = chosen_master_segment[..., 0, :, :]
    master_quadrature = chosen_master_segment[..., 1, :, :]
    cross_re = looks(real_s * master_inphase + imag_s * master_quadrature)
    cross_im = looks(imag_s * master_inphase - real_s * master_quadrature)
    power_sec = looks(real_s * real_s + imag_s * imag_s)
    power_ref = looks(master_inphase * master_inphase + master_quadrature * master_quadrature)
    inverse = 1.0 / jnp.sqrt(power_sec * power_ref + 1e-06)
    return jnp.stack([cross_re * inverse, cross_im * inverse], axis=-3)

def reference(matched_images, master_segment_duo, along_track_whole_displacement, slant_whole_displacement, along_track_subpixel_filter, slant_subpixel_filter, tile_master_segment):
    table = kernel_table()
    segments_real_valued = master_segment_duo.astype(jnp.float32)

    def solitary_matched_result(tile_segment_mask):
        solitary_matched_image, track_displaced, slant_displaced, track_filter_coefficients, slant_filter_coefficients, segment_track_entries = tile_segment_mask
        padded = jnp.pad(solitary_matched_image.astype(jnp.float32), ((0, 0), (HALO, HALO), (0, 0)))
        coregistered = resample(padded, line_weights(track_displaced, track_filter_coefficients, table), line_weights(slant_displaced, slant_filter_coefficients, table))
        segment_chooser = jnp.repeat(segment_track_entries, TILE_HEIGHT)[None, :, None] == 1
        chosen_master_segment = jnp.where(segment_chooser, segments_real_valued[1], segments_real_valued[0])
        return correlation_magnitude(coregistered, chosen_master_segment)
    return lax.map(solitary_matched_result, (matched_images, along_track_whole_displacement, slant_whole_displacement, along_track_subpixel_filter, slant_subpixel_filter, tile_master_segment))
```

```python
import jax
import jax.numpy as jnp
from jax import lax
from jax.experimental import pallas as pl
from jax.experimental.pallas import tpu as pltpu
from jax.sharding import PartitionSpec as P

TAPS = 8
NFRAC = 16
TILE_HEIGHT = 16
F32, BF16 = jnp.float32, jnp.bfloat16
MESH = pl.DeviceIdType.MESH


def kernel_table():
    fraction = jnp.arange(NFRAC, dtype=F32)[:, None] / NFRAC
    distance = jnp.arange(TAPS, dtype=F32)[None, :] - 3.0 - fraction
    kernel_taps = jnp.sinc(distance) * (0.5 + 0.5 * jnp.cos(jnp.pi * distance / 4.0))
    return kernel_taps / jnp.sum(kernel_taps, axis=1, keepdims=True)


def line_weights(shift, index, table):
    onehot = (index[:, :, None] == jnp.arange(NFRAC, dtype=jnp.int32)).astype(F32)
    taps = jnp.sum(onehot[:, :, :, None] * table[None, None], axis=2)
    placed = (
        jnp.arange(16, dtype=jnp.int32)[None, None, None, :]
        == 1 + jnp.arange(TAPS, dtype=jnp.int32)[None, None, :, None] + shift[:, :, None, None]
    )
    weights = jnp.sum(taps[:, :, :, None] * placed.astype(F32), axis=2)
    return jnp.repeat(jnp.swapaxes(weights, 1, 2), TILE_HEIGHT, axis=2)


def split(value):
    high = value.astype(BF16)
    return high, (value - high.astype(F32)).astype(BF16)


def kernel(
    x_hbm, m_ref, azw_ref, rgw_ref, sel_ref, out_ref,
    xs, edge, hsend, halo, mt, xt, ht, y, z, m32, sums, wmat,
    x_sem, e_sem, hs_sem, hr_sem, zs_sem, zr_sem, xs_sem, xr_sem,
):
    acq = lax.axis_index("acq")
    az = lax.axis_index("az")
    zc, xc = acq // 4, acq % 4
    right, left = zc * 4 + (xc + 1) % 4, zc * 4 + (xc + 3) % 4

    for part in range(2):
        rows = pl.ds(112 * (1 - part), 16)
        pltpu.make_async_copy(x_hbm.at[:, :, rows, :], edge.at[part], e_sem.at[part]).start()
    for s in range(8):
        pltpu.make_async_copy(x_hbm.at[s], xs.at[s], x_sem.at[s]).start()

    barrier = pltpu.get_barrier_semaphore()

    def greet(a, b):
        pl.semaphore_signal(barrier, inc=1, device_id=(a, b), device_id_type=MESH)

    greet(right, az)
    greet(left, az)
    pl.when(zc < 3)(lambda: greet(acq + 4, az))
    pl.when(zc > 0)(lambda: greet(acq - 4, az))
    pl.when(az < 15)(lambda: greet(acq, az + 1))
    pl.when(az > 0)(lambda: greet(acq, az - 1))
    for p in range(4):
        mt[acq, p] = m_ref[p // 2, p % 2].T
    many = 2 + jnp.where(zc < 3, 1, 0) + jnp.where(zc > 0, 1, 0)
    many = many + jnp.where(az < 15, 1, 0) + jnp.where(az > 0, 1, 0)
    pl.semaphore_wait(barrier, many)

    def z_copy(block, up):
        return pltpu.make_async_remote_copy(
            src_ref=mt.at[block * 4 + xc], dst_ref=mt.at[block * 4 + xc],
            send_sem=zs_sem.at[up, block], recv_sem=zr_sem.at[block],
            device_id=(acq + 4 if up else acq - 4, az), device_id_type=MESH,
        )

    def x_copy(block, way):
        origin = [xc, xc, (xc + 3) % 4, (xc + 1) % 4][way]
        part = [slice(0, 4), slice(0, 4), slice(0, 2), slice(2, 4)][way]
        ref = mt.at[block * 4 + origin, part]
        return pltpu.make_async_remote_copy(
            src_ref=ref, dst_ref=ref,
            send_sem=xs_sem.at[way, block], recv_sem=xr_sem.at[way, block],
            device_id=(right if way % 2 == 0 else left, az), device_id_type=MESH,
        )

    def h_copy(part):
        return pltpu.make_async_remote_copy(
            src_ref=hsend.at[part], dst_ref=halo.at[pl.ds(64 * part, 64), :],
            send_sem=hs_sem.at[part], recv_sem=hr_sem.at[part],
            device_id=(acq, az + 1 if part == 0 else az - 1), device_id_type=MESH,
        )

    def have(block):
        x_copy(block, 0).start()
        x_copy(block, 1).start()

    def relay(block):
        x_copy(block, 0).wait_recv()
        x_copy(block, 2).start()
        x_copy(block, 1).wait_recv()
        x_copy(block, 3).start()

    def last(block):
        x_copy(block, 2).wait_recv()
        x_copy(block, 3).wait_recv()

    pl.when(zc < 3)(lambda: z_copy(zc, 1).start())
    pl.when(zc > 0)(lambda: z_copy(zc, 0).start())
    have(zc)

    for part in range(2):
        rows = pl.ds(112 * (1 - part), 16)
        pltpu.make_async_copy(x_hbm.at[:, :, rows, :], edge.at[part], e_sem.at[part]).wait()
        for g in range(4):
            picks = []
            for i in range(4):
                sc = 4 * g + i
                tile = edge[part, sc // 2, sc % 2].astype(F32)
                picks.append(tile[12:16] if part == 0 else tile[0:4])
            hsend[part, 16 * g : 16 * g + 16, :] = jnp.concatenate(picks, axis=0).astype(BF16)

        @pl.when(az < 15 if part == 0 else az > 0)
        def _():
            h_copy(part).start()

        @pl.when(az == 0 if part == 0 else az == 15)
        def _():
            halo[64 * part : 64 * part + 64, :] = jnp.zeros((64, 2048), BF16)

    for s in range(8):
        pltpu.make_async_copy(x_hbm.at[s], xs.at[s], x_sem.at[s]).wait()

    @pl.loop(0, 16)
    def _(sc):
        for k in range(16):
            xt[sc, k * 128 : (k + 1) * 128, :] = xs[sc // 2, sc % 2, :, k * 128 : (k + 1) * 128].T

    pl.when(az > 0)(lambda: h_copy(0).wait_recv())
    pl.when(az < 15)(lambda: h_copy(1).wait_recv())

    @pl.loop(0, 16)
    def _(k):
        cols = pl.ds(pl.multiple_of(k * 128, 128), 128)
        ht[cols, :] = halo[:, cols].T

    def z_step(d):
        @pl.when(zc + d <= 3)
        def _():
            z_copy(zc + d, 0).wait_recv()
            pl.when(zc > 0)(lambda: z_copy(zc + d, 0).start())
            have(zc + d)

        @pl.when(zc - d >= 0)
        def _():
            z_copy(zc - d, 1).wait_recv()
            pl.when(zc < 3)(lambda: z_copy(zc - d, 1).start())
            have(zc - d)

    def each(d, step):
        pl.when(zc + d <= 3)(lambda: step(zc + d))
        pl.when(zc - d >= 0)(lambda: step(zc - d))

    zero8 = jnp.zeros((8, 128), F32)
    for c in range(2):
        y[c, 0:8, :] = zero8
        y[c, 2056:2064, :] = zero8
    rows = lax.broadcasted_iota(jnp.int32, (128, 128), 0)
    lanes = lax.broadcasted_iota(jnp.int32, (128, 128), 1)

    @pl.loop(0, 8)
    def _(s):
        @pl.when(s == 0)
        def _():
            relay(zc)
            z_step(1)

        @pl.when(s == 2)
        def _():
            each(1, relay)
            z_step(2)

        @pl.when(s == 4)
        def _():
            each(2, relay)
            z_step(3)

        @pl.when(s == 6)
        def _():
            each(3, relay)

        azw = [azw_ref[s, u : u + 1, :] for u in range(9)]
        own = jnp.zeros((128, 128), F32)
        for u in range(9):
            own = jnp.where(rows - lanes + 4 == u, azw[u], own)
        high, low = split(own)
        for c in range(2):
            base = 8 * s + 4 * c
            top = rows - base
            bottom = rows - 64 - base
            line = jnp.where(
                (top >= 0) & (top < 4),
                top - 4,
                jnp.where((bottom >= 0) & (bottom < 4), 128 + bottom, -100000),
            )
            ends = jnp.zeros((128, 128), F32)
            for u in range(9):
                ends = jnp.where(line - lanes + 4 == u, azw[u], ends)
            ends_high, ends_low = split(ends)
            wmat[c, 0:128, 0:128] = high
            wmat[c, 0:128, 128:256] = low
            wmat[c, 128:256, 0:128] = ends_high
            wmat[c, 128:256, 128:256] = ends_low
        for c in range(2):
            for k in range(8):
                block = slice(k * 256, (k + 1) * 256)
                lhs = jnp.concatenate([xt[2 * s + c, block, :], ht[block, :]], axis=1)
                res = jnp.dot(lhs, wmat[c], preferred_element_type=F32)
                y[c, 8 + k * 256 : 8 + (k + 1) * 256, :] = res[:, 0:128] + res[:, 128:256]
        w = [jnp.broadcast_to(rgw_ref[s, v : v + 1, :], (8, 128)) for v in range(9)]

        @pl.loop(0, 16)
        def _(j):
            base = pl.multiple_of(j * 128, 128)
            psum = None
            for c in range(2):
                win = [y[c, pl.ds(base + 4 + q, 8, stride=16), :] for q in range(8)]
                for k in range(16):
                    win.append(y[c, pl.ds(base + 12 + k, 8, stride=16), :])
                    acc = w[0] * win[k]
                    for v in range(1, 9):
                        acc = acc + w[v] * win[k + v]
                    z[s, j, c, k] = acc
                    sq = acc * acc
                    psum = sq if psum is None else psum + sq
            sums[s, 2, pl.ds(pl.multiple_of(j * 8, 8), 8), :] = psum

    last(zc)
    each(1, last)
    each(2, last)
    each(3, last)

    @pl.loop(0, 16)
    def _(j):
        for p in range(4):
            m32[p] = mt[j, p].astype(F32)
        rowsel = pl.ds(pl.multiple_of(j * 8, 8), 8)
        for m in range(2):
            ps = None
            for k in range(16):
                c = m32[2 * m, pl.ds(k, 8, stride=16), :]
                d = m32[2 * m + 1, pl.ds(k, 8, stride=16), :]
                t = c * c + d * d
                ps = t if ps is None else ps + t
            sums[8, m, rowsel, :] = ps

        @pl.loop(0, 8)
        def _(s):
            sel = jnp.broadcast_to(sel_ref[pl.ds(s, 1), :], (8, 128)) > 0.5
            re = im = None
            for k in range(16):
                at = pl.ds(k, 8, stride=16)
                a = z[s, j, 0, k]
                b = z[s, j, 1, k]
                c = jnp.where(sel, m32[2, at, :], m32[0, at, :])
                d = jnp.where(sel, m32[3, at, :], m32[1, at, :])
                t = a * c + b * d
                q = b * c - a * d
                re = t if re is None else re + t
                im = q if im is None else im + q
            sums[s, 0, rowsel, :] = re
            sums[s, 1, rowsel, :] = im

    e = (
        lax.broadcasted_iota(jnp.int32, (32, 128), 0)
        == lax.broadcasted_iota(jnp.int32, (32, 128), 1) // 4
    ).astype(BF16)

    def group(p):
        high, low = split(p)
        dn = (((1,), (1,)), ((), ()))
        return lax.dot_general(e, high, dn, preferred_element_type=F32) + lax.dot_general(
            e, low, dn, preferred_element_type=F32
        )

    @pl.loop(0, 8)
    def _(s):
        sel = sel_ref[pl.ds(s, 1), :] > 0.5
        pref = group(jnp.where(sel, sums[8, 1], sums[8, 0]))
        inverse = 1.0 / jnp.sqrt(group(sums[s, 2]) * pref + 1e-6)
        out_ref[s, 0] = group(sums[s, 0]) * inverse
        out_ref[s, 1] = group(sums[s, 1]) * inverse

    pl.when(az < 15)(lambda: h_copy(0).wait_send())
    pl.when(az > 0)(lambda: h_copy(1).wait_send())
    for block in range(4):
        pl.when((zc < 3) & (block <= zc))(lambda: z_copy(block, 1).wait_send())
        pl.when((zc > 0) & (block >= zc))(lambda: z_copy(block, 0).wait_send())
        for way in range(4):
            x_copy(block, way).wait_send()


def on_device(images, masters, az_shift, rg_shift, az_index, rg_index, segment):
    table = kernel_table()
    azw = line_weights(az_shift, az_index, table)
    rgw = line_weights(rg_shift, rg_index, table)
    sel = jnp.repeat(segment, TILE_HEIGHT, axis=1).astype(F32)
    vmem = pl.BlockSpec(memory_space=pltpu.VMEM)
    dma = pltpu.SemaphoreType.DMA
    return pl.pallas_call(
        kernel,
        out_shape=jax.ShapeDtypeStruct((8, 2, 32, 128), F32),
        in_specs=[pl.BlockSpec(memory_space=pl.ANY)] + [vmem] * 4,
        out_specs=vmem,
        scratch_shapes=[
            pltpu.VMEM((8, 2, 128, 2048), BF16),
            pltpu.VMEM((2, 8, 2, 16, 2048), BF16),
            pltpu.VMEM((2, 64, 2048), BF16),
            pltpu.VMEM((128, 2048), BF16),
            pltpu.VMEM((16, 4, 128, 128), BF16),
            pltpu.VMEM((16, 2048, 128), BF16),
            pltpu.VMEM((2048, 128), BF16),
            pltpu.VMEM((2, 2064, 128), F32),
            pltpu.VMEM((8, 16, 2, 16, 8, 128), F32),
            pltpu.VMEM((4, 128, 128), F32),
            pltpu.VMEM((9, 3, 128, 128), F32),
            pltpu.VMEM((2, 256, 256), BF16),
            dma((8,)),
            dma((2,)),
            dma((2,)),
            dma((2,)),
            dma((2, 4)),
            dma((4,)),
            dma((4, 4)),
            dma((4, 4)),
        ],
        compiler_params=pltpu.CompilerParams(
            collective_id=0, has_side_effects=True, vmem_limit_bytes=58 * 2**20
        ),
        name="resample",
    )(images, masters, azw, rgw, sel)


def solution(mesh):
    return jax.shard_map(
        on_device,
        mesh=mesh,
        in_specs=(
            P("acq", None, "az", None),
            P(None, None, "az", "acq"),
            P("acq", "az"),
            P("acq", "az"),
            P("acq", "az"),
            P("acq", "az"),
            P("acq", "az"),
        ),
        out_specs=P("acq", None, "az", None),
        check_vma=False,
    )
```

```python
import numpy as np

import jax
import jax.numpy as jnp
from jax import lax
from jax.experimental import pallas as pl
from jax.experimental.pallas import tpu as pltpu
from jax.sharding import PartitionSpec as P

MESH = pl.DeviceIdType.MESH
F32, BF16 = jnp.float32, jnp.bfloat16
TAPS, NFRAC = 8, 16
R = 512
NB = R // 128
HEAD = 24


def filter_table():
    x = np.arange(TAPS)[None, :] - 3.0 - np.arange(NFRAC)[:, None] / NFRAC
    taps = np.sinc(x) * (0.5 + 0.5 * np.cos(np.pi * x / 4.0))
    return taps / taps.sum(axis=1, keepdims=True)


def split(value):
    high = value.astype(BF16)
    return high, (value - high.astype(F32)).astype(BF16)


def spread(ints):
    block = lax.broadcasted_iota(jnp.int32, (8, 128), 1) // 16
    out = jnp.zeros((8, 128), F32)
    for b in range(8):
        out = jnp.where(block == b, ints[:, b : b + 1].astype(F32), out)
    return out


def pick(index, column):
    out = jnp.full((8, 128), float(column[0]), F32)
    for f in range(1, NFRAC):
        out = jnp.where(index == float(f), float(column[f]), out)
    return out


def build_weights(i0, i1, i2, i3, i4, azw, rgw, flag):
    table = filter_table()
    az_back = spread(i0[...]) < -0.5
    az_index = spread(i2[...])
    rg_index = spread(i3[...])
    centre = pick(rg_index, table[:, 3])
    taps = [pick(az_index, table[:, t]) * centre for t in range(TAPS)]
    zero = jnp.zeros((8, 128), F32)
    for u in range(TAPS + 1):
        azw[u] = jnp.where(az_back, taps[u] if u < TAPS else zero, taps[u - 1] if u > 0 else zero)
    for t in range(TAPS):
        rgw[t] = pick(rg_index, table[:, t] / table[:, 3])
    flag[0] = spread(i1[...])
    flag[1] = spread(i4[...])


def build_matrices(azw, wmat):
    rows = lax.broadcasted_iota(jnp.int32, (128, 128), 0)
    lanes = lax.broadcasted_iota(jnp.int32, (128, 128), 1)
    trow = lax.broadcasted_iota(jnp.int32, (16, 128), 0)
    tlane = lax.broadcasted_iota(jnp.int32, (16, 128), 1)

    @pl.loop(0, 8)
    def _(s):
        weight = [azw[u, pl.ds(s, 1), :] for u in range(9)]

        def banded(offset):
            out = jnp.zeros(offset.shape, F32)
            for u in range(9):
                out = jnp.where(offset == u - 4, weight[u], out)
            return split(out)

        high, low = banded(rows - lanes)
        half = 8 * (s % 2)
        start = pl.multiple_of(16 * (s // 2), 16)
        for c in range(2):
            n = 2 * s + c
            wmat[n, 0:128, 0:128] = high
            wmat[n, 0:128, 128:256] = low
            wmat[n, 128:256, :] = jnp.zeros((128, 256), BF16)
            at = trow - half - 4 * c
            for side in range(2):
                line = jnp.where((at >= 0) & (at < 4), at + (-4, 128)[side], -1000)
                high_end, low_end = banded(line - tlane)
                block = pl.ds(128 + 64 * side + start, 16)
                wmat[n, block, 0:128] = high_end
                wmat[n, block, 128:256] = low_end


def azimuth(j, buf, xt, ht, wmat, s, c):
    n = 2 * s + c
    rows = pl.ds(pl.multiple_of(j * R, R), R)
    lhs = jnp.concatenate([xt[n, rows, :], ht[rows, :]], axis=1)
    res = jnp.dot(lhs, wmat[n], preferred_element_type=F32)
    buf[c, pl.ds(8 * HEAD + s, R, stride=8), :] = res[:, 0:128] + res[:, 128:256]


def carry(src, dst):
    for c in range(2):
        dst[c, 0 : 8 * HEAD, :] = src[c, 8 * R : 8 * (R + HEAD), :]


class Range:
    def __init__(self, j, buf, z, sums, rgw, flag):
        self.j, self.buf, self.z, self.sums = j, buf, z, sums
        self.w = [rgw[t] for t in range(TAPS)]
        self.back = flag[0] < -0.5
        self.raw = [None, None]
        self.win = [[], []]

    def need(self, c, q):
        row = self.buf[c, pl.ds(self.base + 8 * q, 8), :]
        before = self.raw[c] if self.raw[c] is not None else self.buf[c, pl.ds(self.base + 8 * q - 8, 8), :]
        self.raw[c] = row
        self.win[c] = (self.win[c] + [jnp.where(self.back, before, row)])[-8:]

    def box(self, i, first=8):
        psum = None
        w = self.w
        self.base = pl.multiple_of(i * 128, 128)
        for c in range(2):
            for k in range(16):
                q = first + k
                if not self.win[c]:
                    for d in range(-3, 4):
                        self.need(c, q + d)
                self.need(c, q + 4)
                win = self.win[c]
                acc = win[3]
                for t in (0, 1, 2, 4, 5, 6, 7):
                    acc = acc + w[t] * win[t]
                self.z[c, R * self.j + 16 * i + k] = acc
                sq = acc * acc
                psum = sq if psum is None else psum + sq
        self.sums[2, R // 16 * self.j + i] = psum


def resample(refs, hook):
    xt, ht, wmat, buf_a, buf_b, z, sums, rgw, flag = refs

    def half(j, cur, nxt):
        carry(cur, nxt)

        @pl.loop(0, 8)
        def _(i):
            hook(j, i)
            azimuth(j + 1, nxt, xt, ht, wmat, i, 0)
            azimuth(j + 1, nxt, xt, ht, wmat, i, 1)
            for b in range(NB):
                Range(j, cur, z, sums, rgw, flag).box(i * NB + b)

    for c in range(2):
        buf_a[c, 0 : 8 * HEAD, :] = jnp.zeros((8 * HEAD, 128), F32)

    @pl.loop(0, 8)
    def _(i):
        azimuth(0, buf_a, xt, ht, wmat, i, 0)
        azimuth(0, buf_a, xt, ht, wmat, i, 1)

    n = 2048 // R
    for p in range(n // 2 - 1):
        half(2 * p, buf_a, buf_b)
        half(2 * p + 1, buf_b, buf_a)
    half(n - 2, buf_a, buf_b)
    last = buf_b

    @pl.loop(0, 8 * NB)
    def _(i):
        Range(n - 1, last, z, sums, rgw, flag).box(i)

    for c in range(2):
        buf_a[c, 0 : 8 * HEAD, :] = last[c, 8 * R : 8 * (R + HEAD), :]
        buf_a[c, 8 * HEAD : 8 * (HEAD + 8), :] = jnp.zeros((64, 128), F32)
    Range(n, buf_a, z, sums, rgw, flag).box(0)


def cross_slab(j, mt, m32, mp, z, sums, flag):
    sel = flag[1] > 0.5

    def row(ref, r):
        return jnp.broadcast_to(ref[pl.ds(r, 1), :], (8, 128))

    for p in range(4):
        m32[p] = mt[j, p].astype(F32)
    for m in range(2):
        t = m32[2 * m] * m32[2 * m] + m32[2 * m + 1] * m32[2 * m + 1]
        mp[m] = jnp.sum(t.reshape(8, 16, 128), axis=1)

    @pl.loop(0, 8)
    def _(i):
        box = j * 8 + i
        sums[3, box + 1] = jnp.where(sel, row(mp.at[1], i), row(mp.at[0], i))
        re = im = None
        for k in range(16):
            r = 16 * i + k
            a = z[0, box * 16 + 16 + k]
            b = z[1, box * 16 + 16 + k]
            c = jnp.where(sel, row(m32.at[2], r), row(m32.at[0], r))
            d = jnp.where(sel, row(m32.at[3], r), row(m32.at[1], r))
            t = a * c + b * d
            q = b * c - a * d
            re = t if re is None else re + t
            im = q if im is None else im + q
        sums[0, box + 1] = re
        sums[1, box + 1] = im


def finish(sums, out_ref):
    e = (
        lax.broadcasted_iota(jnp.int32, (32, 128), 0)
        == lax.broadcasted_iota(jnp.int32, (32, 128), 1) // 4
    ).astype(BF16)
    dn = (((1,), (1,)), ((), ()))

    def group(q, s):
        flat = sums.at[q].reshape(129 * 8, 128)
        high, low = split(flat[pl.ds(8 + s, 128, stride=8), :])
        return lax.dot_general(e, high, dn, preferred_element_type=F32) + lax.dot_general(
            e, low, dn, preferred_element_type=F32
        )

    @pl.loop(0, 8)
    def _(s):
        g = [group(q, s) for q in range(4)]
        inverse = 1.0 / jnp.sqrt(g[2] * g[3] + 1e-6)
        out_ref[s, 0] = g[0] * inverse
        out_ref[s, 1] = g[1] * inverse

def kernel(
    x_hbm, m_ref, i0, i1, i2, i3, i4, out_ref,
    xs, edge, hsend, halo, mt, xt, ht, buf_a, buf_b, z, m32, mp, sums, azw, rgw, flag, wmat,
    x_sem, e_sem, hs_sem, hr_sem, zs_sem, zr_sem, xs_sem, xr_sem,
):
    acq = lax.axis_index("acq")
    az = lax.axis_index("az")
    zc, xc = acq // 4, acq % 4
    right, left = zc * 4 + (xc + 1) % 4, zc * 4 + (xc + 3) % 4
    inner = (zc == 1) | (zc == 2)
    low = zc < 2
    order = [
        zc,
        jnp.where(low, zc + 1, zc - 1),
        jnp.where(inner, jnp.where(low, 0, 3), jnp.where(low, 2, 1)),
        jnp.where(low, 3, 0),
    ]

    def edge_copy(part):
        rows = pl.ds(112 * (1 - part), 16)
        return pltpu.make_async_copy(x_hbm.at[:, :, rows, :], edge.at[part], e_sem.at[part])

    def x_load(s):
        return pltpu.make_async_copy(x_hbm.at[s], xs.at[s], x_sem.at[s])

    for part in range(2):
        edge_copy(part).start()
    for s in range(8):
        x_load(s).start()

    barrier = pltpu.get_barrier_semaphore()

    def greet(a, b):
        pl.semaphore_signal(barrier, inc=1, device_id=(a, b), device_id_type=MESH)

    greet(right, az)
    greet(left, az)
    for g in range(1, 4):
        greet(order[g] * 4 + xc, az)
    pl.when(az < 15)(lambda: greet(acq, az + 1))
    pl.when(az > 0)(lambda: greet(acq, az - 1))
    for p in range(4):
        mt[acq, p] = m_ref[p // 2, p % 2].T

    def z_copy(block):
        return pltpu.make_async_remote_copy(
            src_ref=mt.at[acq], dst_ref=mt.at[acq],
            send_sem=zs_sem.at[block], recv_sem=zr_sem.at[zc],
            device_id=(block * 4 + xc, az), device_id_type=MESH,
        )

    def z_wait(block):
        pltpu.make_async_remote_copy(
            src_ref=mt.at[acq], dst_ref=mt.at[block * 4 + xc],
            send_sem=zs_sem.at[block], recv_sem=zr_sem.at[block],
            device_id=(block * 4 + xc, az), device_id_type=MESH,
        ).wait_recv()

    def x_copy(block, way):
        origin = [xc, xc, (xc + 3) % 4, (xc + 1) % 4][way]
        part = [slice(0, 4), slice(0, 4), slice(0, 2), slice(2, 4)][way]
        ref = mt.at[block * 4 + origin, part]
        return pltpu.make_async_remote_copy(
            src_ref=ref, dst_ref=ref,
            send_sem=xs_sem.at[way, block], recv_sem=xr_sem.at[way, block],
            device_id=(right if way % 2 == 0 else left, az), device_id_type=MESH,
        )

    def h_copy(part):
        return pltpu.make_async_remote_copy(
            src_ref=hsend.at[part], dst_ref=halo.at[pl.ds(64 * part, 64), :],
            send_sem=hs_sem.at[part], recv_sem=hr_sem.at[part],
            device_id=(acq, az + 1 if part == 0 else az - 1), device_id_type=MESH,
        )

    def have(block):
        x_copy(block, 0).start()
        x_copy(block, 1).start()

    def relay(block):
        x_copy(block, 0).wait_recv()
        x_copy(block, 2).start()
        x_copy(block, 1).wait_recv()
        x_copy(block, 3).start()

    def last(block):
        x_copy(block, 2).wait_recv()
        x_copy(block, 3).wait_recv()

    for part in range(2):
        edge_copy(part).wait()
        for g in range(4):
            picks = []
            for i in range(4):
                sc = 4 * g + i
                tile = edge[part, sc // 2, sc % 2].astype(F32)
                picks.append(tile[12:16] if part == 0 else tile[0:4])
            hsend[part, 16 * g : 16 * g + 16, :] = jnp.concatenate(picks, axis=0).astype(BF16)

    many = 5 + jnp.where(az < 15, 1, 0) + jnp.where(az > 0, 1, 0)
    pl.semaphore_wait(barrier, many)
    for part in range(2):

        @pl.when(az < 15 if part == 0 else az > 0)
        def _():
            h_copy(part).start()

        @pl.when(az == 0 if part == 0 else az == 15)
        def _():
            halo[64 * part : 64 * part + 64, :] = jnp.zeros((64, 2048), BF16)

    for g in range(1, 4):
        z_copy(order[g]).start()
    have(zc)

    build_weights(i0, i1, i2, i3, i4, azw, rgw, flag)
    build_matrices(azw, wmat)

    @pl.loop(0, 8)
    def _(s):
        x_load(s).wait()

        @pl.loop(0, 2)
        def _(c):
            for k in range(16):
                xt[2 * s + c, k * 128 : (k + 1) * 128, :] = xs[s, c, :, k * 128 : (k + 1) * 128].T

    z_wait(order[1])
    have(order[1])
    relay(order[0])
    pl.when(az > 0)(lambda: h_copy(0).wait_recv())
    pl.when(az < 15)(lambda: h_copy(1).wait_recv())

    @pl.loop(0, 4)
    def _(k):
        for i in range(4):
            cols = pl.ds(pl.multiple_of(k * 512 + i * 128, 128), 128)
            ht[cols, :] = halo[:, cols].T

    def step_a():
        z_wait(order[2])
        have(order[2])

    def step_b():
        z_wait(order[3])
        have(order[3])

    steps = {
        0: ((0, step_a), (4, lambda: relay(order[1]))),
        1: ((0, step_b), (4, lambda: relay(order[2]))),
        2: ((4, lambda: relay(order[3])),),
    }

    def hook(j, i):
        for at, step in steps.get(j, ()):
            pl.when(i == at)(step)

    resample((xt, ht, wmat, buf_a, buf_b, z, sums, rgw, flag), hook)

    @pl.loop(0, 4)
    def _(g):
        block = jnp.where(
            g < 2, jnp.where(g == 0, order[0], order[1]), jnp.where(g == 2, order[2], order[3])
        )
        last(block)

        @pl.loop(0, 4)
        def _(x):
            cross_slab(block * 4 + x, mt, m32, mp, z, sums, flag)

    finish(sums, out_ref)

    pl.when(az < 15)(lambda: h_copy(0).wait_send())
    pl.when(az > 0)(lambda: h_copy(1).wait_send())
    for g in range(1, 4):
        z_copy(order[g]).wait_send()
    for block in range(4):
        for way in range(4):
            x_copy(block, way).wait_send()


def on_device(images, masters, az_shift, rg_shift, az_index, rg_index, segment):
    vmem = pl.BlockSpec(memory_space=pltpu.VMEM)
    dma = pltpu.SemaphoreType.DMA
    return pl.pallas_call(
        kernel,
        out_shape=jax.ShapeDtypeStruct((8, 2, 32, 128), F32),
        in_specs=[pl.BlockSpec(memory_space=pl.ANY)] + [vmem] * 6,
        out_specs=vmem,
        scratch_shapes=[
            pltpu.VMEM((8, 2, 128, 2048), BF16),
            pltpu.VMEM((2, 8, 2, 16, 2048), BF16),
            pltpu.VMEM((2, 64, 2048), BF16),
            pltpu.VMEM((128, 2048), BF16),
            pltpu.VMEM((16, 4, 128, 128), BF16),
            pltpu.VMEM((16, 2048, 128), BF16),
            pltpu.VMEM((2048, 128), BF16),
            pltpu.VMEM((2, 8 * (R + HEAD), 128), F32),
            pltpu.VMEM((2, 8 * (R + HEAD), 128), F32),
            pltpu.VMEM((2, 2064, 8, 128), F32),
            pltpu.VMEM((4, 128, 128), F32),
            pltpu.VMEM((2, 8, 128), F32),
            pltpu.VMEM((4, 129, 8, 128), F32),
            pltpu.VMEM((9, 8, 128), F32),
            pltpu.VMEM((8, 8, 128), F32),
            pltpu.VMEM((2, 8, 128), F32),
            pltpu.VMEM((16, 256, 256), BF16),
            dma((8,)),
            dma((2,)),
            dma((2,)),
            dma((2,)),
            dma((4,)),
            dma((4,)),
            dma((4, 4)),
            dma((4, 4)),
        ],
        compiler_params=pltpu.CompilerParams(
            collective_id=0, has_side_effects=True, vmem_limit_bytes=60 * 2**20
        ),
        name="resample",
    )(images, masters, az_shift, rg_shift, az_index, rg_index, segment)


def solution(mesh):
    return jax.shard_map(
        on_device,
        mesh=mesh,
        in_specs=(
            P("acq", None, "az", None),
            P(None, None, "az", "acq"),
            P("acq", "az"),
            P("acq", "az"),
            P("acq", "az"),
            P("acq", "az"),
            P("acq", "az"),
        ),
        out_specs=P("acq", None, "az", None),
        check_vma=False,
    )
```

```python
import numpy as np

import jax
import jax.numpy as jnp
from jax import lax
from jax.experimental import pallas as pl
from jax.experimental.pallas import tpu as pltpu
from jax.sharding import PartitionSpec as P

MESH = pl.DeviceIdType.MESH
F32, BF16 = jnp.float32, jnp.bfloat16
TAPS, NFRAC = 8, 16
CHUNKS = 4
BOXES = 2


def filter_table():
    x = np.arange(TAPS)[None, :] - 3.0 - np.arange(NFRAC)[:, None] / NFRAC
    taps = np.sinc(x) * (0.5 + 0.5 * np.cos(np.pi * x / 4.0))
    return taps / taps.sum(axis=1, keepdims=True)


def split(value):
    high = value.astype(BF16)
    return high, (value - high.astype(F32)).astype(BF16)


def spread(ints):
    block = lax.broadcasted_iota(jnp.int32, (8, 128), 1) // 16
    out = jnp.zeros((8, 128), F32)
    for b in range(8):
        out = jnp.where(block == b, ints[:, b : b + 1].astype(F32), out)
    return out


def pick(index, column):
    out = jnp.full((8, 128), float(column[0]), F32)
    for f in range(1, NFRAC):
        out = jnp.where(index == float(f), float(column[f]), out)
    return out


def across(ints):
    lane = lax.broadcasted_iota(jnp.int32, (8, 128), 1)
    row = lax.broadcasted_iota(jnp.int32, (8, 128), 0)
    value = ints.astype(F32)
    both = jnp.where(lane % 8 < 4, value[:, 0:1], value[:, 7:8])
    mine = jnp.where(lane // 8 % 8 == row, both, 0.0)
    return jnp.broadcast_to(jnp.sum(mine, axis=0, keepdims=True), (8, 128))


def place(back, taps):
    zero = jnp.zeros((8, 128), F32)
    return [
        jnp.where(back, taps[u] if u < TAPS else zero, taps[u - 1] if u > 0 else zero)
        for u in range(TAPS + 1)
    ]


def build_weights(i0, i1, i2, i3, i4, azw, rgw, flag, eazw, ergw):
    table = filter_table()
    rg_index = spread(i3[...])
    az_index = spread(i2[...])
    centre = pick(rg_index, table[:, 3])
    taps = place(spread(i0[...]) < -0.5, [pick(az_index, table[:, t]) * centre for t in range(TAPS)])
    for u in range(TAPS + 1):
        azw[u] = taps[u]
    for t in range(TAPS):
        rgw[t] = pick(rg_index, table[:, t] / table[:, 3])
    flag[0] = spread(i1[...])
    flag[1] = spread(i4[...])
    flag[2] = across(i4[...])
    rg_index = across(i3[...])
    az_index = across(i2[...])
    taps = place(across(i0[...]) < -0.5, [pick(az_index, table[:, t]) for t in range(TAPS)])
    more = place(across(i1[...]) < -0.5, [pick(rg_index, table[:, t]) for t in range(TAPS)])
    for u in range(TAPS + 1):
        eazw[u] = taps[u]
        ergw[u] = more[u]


def azimuth_own(xs, xt_a, xt_b, y, azw, wait, steps):
    rows = lax.broadcasted_iota(jnp.int32, (128, 128), 0)
    lanes = lax.broadcasted_iota(jnp.int32, (128, 128), 1)
    for c in range(2):
        y[c, 0:64, :] = jnp.zeros((64, 128), F32)
        y[c, 8 * 2056 : 8 * 2064, :] = jnp.zeros((64, 128), F32)

    def turn(s, dst):
        for c in range(2):
            for k in range(16):
                part = slice(k * 128, (k + 1) * 128)
                dst[c, part, :] = xs[s, c, :, part].T

    def half(s, cur, nxt):
        pl.when(s < 7)(lambda: wait(s + 1))
        offset = rows - lanes
        own = jnp.zeros((128, 128), F32)
        for u in range(9):
            own = jnp.where(offset == u - 4, azw[u, pl.ds(s, 1), :], own)
        matrix = jnp.concatenate(split(own), axis=0)
        for c in range(2):
            for k in range(CHUNKS):
                n = 2048 // CHUNKS
                lhs = cur[c, k * n : (k + 1) * n, :]
                y[c, pl.ds(64 + 8 * n * k + s, n, stride=8), :] = jnp.dot(
                    jnp.concatenate([lhs, lhs], axis=1), matrix, preferred_element_type=F32
                )
        turn(jnp.minimum(s + 1, 7), nxt)

    wait(0)
    turn(0, xt_a)

    start = 0
    for stop, step in steps:

        @pl.loop(start, stop)
        def _(p):
            half(2 * p, xt_a, xt_b)
            half(2 * p + 1, xt_b, xt_a)

        step()
        start = stop


def range_filter(y, z, sums, rgw, flag, edge, et, steps):
    w = [rgw[t] for t in range(TAPS)]

    def boxes(i):
        back = flag[0] < -0.5
        base = pl.multiple_of(i * (128 * BOXES), 128)
        cols = pl.ds(pl.multiple_of(i % 16 * 128, 128), 128)
        block = edge[i // 32, pl.ds(i // 16 % 2 * 4, 4), :, :, cols].reshape(128, 128)
        et[i // 16, cols, :] = block.T
        psum = [None] * BOXES
        for c in range(2):

            def load(q):
                return y[c, pl.ds(base + 64 + 8 * q, 8), :]

            before, win = load(-4), []
            for q in range(-3, 16 * BOXES + 4):
                row = load(q)
                win = (win + [jnp.where(back, before, row)])[-8:]
                before = row
                k = q - 4
                if k < 0:
                    continue
                acc = win[3]
                for t in (0, 1, 2, 4, 5, 6, 7):
                    acc = acc + w[t] * win[t]
                z[c, 16 * BOXES * i + k] = acc
                sq = acc * acc
                b = k // 16
                psum[b] = sq if psum[b] is None else psum[b] + sq
        for b in range(BOXES):
            sums[2, BOXES * i + b] = psum[b]

    start = 0
    for stop, step in steps:
        pl.loop(start, stop)(boxes)
        step()
        start = stop


def edge_line(lane):
    return jnp.where(lane % 8 < 4, lane % 8, 120 + lane % 8)


def edge_matrices(eazw, ewm, gmat):
    row = lax.broadcasted_iota(jnp.int32, (128, 128), 0)
    lane = lax.broadcasted_iota(jnp.int32, (128, 128), 1)
    image = lane // 8 % 8 * 2 + lane // 64
    at = edge_line(lane)

    def banded(line, owner, where):
        offset = jnp.where(owner == image, line - at, 1000)
        out = jnp.zeros((128, 128), F32)
        for u in range(9):
            out = jnp.where(offset == u - 4, eazw[u, 0:1, :], out)
        high, low = split(out)
        ewm[where, 0:128] = high
        ewm[where, 128:256] = low

    for q in range(4):
        banded(row % 16 + (112 if q < 2 else 0), q % 2 * 8 + row // 16, slice(128 * q, 128 * q + 128))
    banded(jnp.where(row < 64, row % 4 - 4, 128 + row % 4), row % 64 // 4, slice(512, 640))
    hit = (row == at).astype(F32)
    left = lane < 64
    zero = jnp.zeros((128, 128), F32)
    gmat[0:128, 0:128] = jnp.where(left, hit, zero).astype(BF16)
    gmat[128:256, 0:128] = jnp.where(left, zero, hit).astype(BF16)
    gmat[0:128, 128:256] = jnp.where(left, zero, hit).astype(BF16)
    gmat[128:256, 128:256] = jnp.where(left, -hit, zero).astype(BF16)


def edge_filter(halo, et, ewm, ye, ze, ergw):
    @pl.loop(0, 4)
    def _(k):
        for i in range(4):
            cols = pl.ds(pl.multiple_of(k * 512 + i * 128, 128), 128)
            et[4, cols, :] = halo[:, cols].T

    for k in range(2):
        part = slice(1024 * k, 1024 * k + 1024)
        lhs = jnp.concatenate([et[q, part, :] for q in range(5)], axis=1)
        res = jnp.dot(lhs, ewm[...], preferred_element_type=F32)
        ye[8 + 1024 * k : 8 + 1024 * k + 1024, :] = res[:, 0:128] + res[:, 128:256]
    ye[0:8, :] = jnp.zeros((8, 128), F32)
    ye[2056:2064, :] = jnp.zeros((8, 128), F32)

    @pl.loop(0, 32)
    def _(k):
        base = pl.multiple_of(k * 64, 64)
        acc = ergw[0, 0:1, :] * ye[pl.ds(base + 4, 64), :]
        for u in range(1, 9):
            acc = acc + ergw[u, 0:1, :] * ye[pl.ds(base + 4 + u, 64), :]
        ze[pl.ds(base, 64), :] = acc


def edge_cross(j, mt, gmat, ze, esum, flag):
    sel = flag[2, 0:1, :] > 0.5
    m = [
        jnp.dot(
            jnp.concatenate([mt[j, 2 * q], mt[j, 2 * q + 1]], axis=1),
            gmat[...],
            preferred_element_type=F32,
        )
        for q in range(2)
    ]
    one = jnp.where(sel, m[1][:, 0:128], m[0][:, 0:128])
    two = jnp.where(sel, m[1][:, 128:256], m[0][:, 128:256])
    v = ze[pl.ds(pl.multiple_of(j * 128, 128), 128), :]
    for q, product in enumerate((v * one, v * two, v * v, one * one)):
        esum[q, pl.ds(pl.multiple_of(j * 8, 8), 8), :] = jnp.sum(product.reshape(8, 16, 128), axis=1)


def cross_slab(j, mt, m32, mp, z, sums, flag):
    sel = flag[1] > 0.5

    def row(ref, r):
        return jnp.broadcast_to(ref[pl.ds(r, 1), :], (8, 128))

    for q in range(2):
        rows = slice(128 * q, 128 * q + 128)
        for p in range(4):
            m32[p, rows] = mt[j + q, p].astype(F32)
        for m in range(2):
            t = m32[2 * m, rows] * m32[2 * m, rows] + m32[2 * m + 1, rows] * m32[2 * m + 1, rows]
            mp[m, 8 * q : 8 * q + 8] = jnp.sum(t.reshape(8, 16, 128), axis=1)

    @pl.loop(0, 8)
    def _(h):
        for i in (2 * h, 2 * h + 1):
            box = j * 8 + i
            sums[3, box] = jnp.where(sel, row(mp.at[1], i), row(mp.at[0], i))
            re = im = None
            for k in range(16):
                r = 16 * i + k
                a = z[0, box * 16 + k]
                b = z[1, box * 16 + k]
                c = jnp.where(sel, row(m32.at[2], r), row(m32.at[0], r))
                d = jnp.where(sel, row(m32.at[3], r), row(m32.at[1], r))
                t = a * c + b * d
                q = b * c - a * d
                re = t if re is None else re + t
                im = q if im is None else im + q
            sums[0, box] = re
            sums[1, box] = im


def finish(sums, esum, out_ref):
    dn = (((1,), (1,)), ((), ()))

    def folded(e, value):
        high, low = split(value)
        return lax.dot_general(e, high, dn, preferred_element_type=F32) + lax.dot_general(
            e, low, dn, preferred_element_type=F32
        )

    row = lax.broadcasted_iota(jnp.int32, (32, 128), 0)
    lane = lax.broadcasted_iota(jnp.int32, (32, 128), 1)
    lines = (row == lane // 4).astype(BF16)

    @pl.loop(0, 2)
    def _(p):
        for s in (4 * p, 4 * p + 1, 4 * p + 2, 4 * p + 3):
            g = [
                folded(lines, sums.at[q].reshape(1024, 128)[pl.ds(s, 128, stride=8), :])
                for q in range(4)
            ]
            inverse = 1.0 / jnp.sqrt(g[2] * g[3] + 1e-6)
            out_ref[s, 0] = g[0] * inverse
            out_ref[s, 1] = g[1] * inverse

    ends = ((row // 2 == lane // 8 % 8) & (row % 2 == lane % 8 // 4)).astype(BF16)
    g = [folded(ends, esum[q]) for q in range(4)]
    inverse = 1.0 / jnp.sqrt(g[2] * g[3] + 1e-6)
    for part in range(2):
        value = g[part] * inverse
        for s in range(8):
            out_ref[s, part, 0:1, :] = value[2 * s : 2 * s + 1, :]
            out_ref[s, part, 31:32, :] = value[2 * s + 1 : 2 * s + 2, :]

def kernel(
    x_hbm, m_ref, i0, i1, i2, i3, i4, out_ref,
    hsend, halo, mt,
    xs, edge, xt_a, xt_b, y, z, et, ye, ze, m32, mp, sums, esum, azw, rgw, flag, eazw, ergw, ewm, gmat,
    x_sem, e_sem, hs_sem, hr_sem, zs_sem, zr_sem, xs_sem, xr_sem,
):
    acq = lax.axis_index("acq")
    az = lax.axis_index("az")
    zc, xc = acq // 4, acq % 4
    right, left = zc * 4 + (xc + 1) % 4, zc * 4 + (xc + 3) % 4
    inner = (zc == 1) | (zc == 2)
    low = zc < 2
    order = [
        zc,
        jnp.where(low, zc + 1, zc - 1),
        jnp.where(inner, jnp.where(low, 0, 3), jnp.where(low, 2, 1)),
        jnp.where(low, 3, 0),
    ]

    def edge_copy(part):
        rows = pl.ds(112 * (1 - part), 16)
        return pltpu.make_async_copy(x_hbm.at[:, :, rows, :], edge.at[part], e_sem.at[part])

    def x_load(s):
        return pltpu.make_async_copy(x_hbm.at[s], xs.at[s], x_sem.at[s])

    for part in range(2):
        edge_copy(part).start()
    for s in range(8):
        x_load(s).start()

    barrier = pltpu.get_barrier_semaphore()

    def greet(a, b):
        pl.semaphore_signal(barrier, inc=1, device_id=(a, b), device_id_type=MESH)

    greet(right, az)
    greet(left, az)
    pl.when(zc < 3)(lambda: greet(acq + 4, az))
    pl.when(zc > 0)(lambda: greet(acq - 4, az))
    pl.when(az < 15)(lambda: greet(acq, az + 1))
    pl.when(az > 0)(lambda: greet(acq, az - 1))
    for p in range(4):
        mt[acq, p] = m_ref[p // 2, p % 2].T

    def z_copy(block, up):
        ref = mt.at[block * 4 + xc]
        return pltpu.make_async_remote_copy(
            src_ref=ref, dst_ref=ref,
            send_sem=zs_sem.at[up, block], recv_sem=zr_sem.at[block],
            device_id=(acq + 4 if up else acq - 4, az), device_id_type=MESH,
        )

    def x_copy(block, way):
        origin = [xc, xc, (xc + 3) % 4, (xc + 1) % 4][way]
        part = [slice(0, 4), slice(0, 4), slice(0, 2), slice(2, 4)][way]
        ref = mt.at[block * 4 + origin, part]
        return pltpu.make_async_remote_copy(
            src_ref=ref, dst_ref=ref,
            send_sem=xs_sem.at[way, block], recv_sem=xr_sem.at[way, block],
            device_id=(right if way % 2 == 0 else left, az), device_id_type=MESH,
        )

    def h_copy(part):
        return pltpu.make_async_remote_copy(
            src_ref=hsend.at[part], dst_ref=halo.at[pl.ds(64 * part, 64), :],
            send_sem=hs_sem.at[part], recv_sem=hr_sem.at[part],
            device_id=(acq, az + 1 if part == 0 else az - 1), device_id_type=MESH,
        )

    def have(block):
        x_copy(block, 0).start()
        x_copy(block, 1).start()

    def relay(block):
        x_copy(block, 0).wait_recv()
        x_copy(block, 2).start()
        x_copy(block, 1).wait_recv()
        x_copy(block, 3).start()

    def last(block):
        x_copy(block, 2).wait_recv()
        x_copy(block, 3).wait_recv()

    for part in range(2):
        edge_copy(part).wait()
        for g in range(4):
            picks = []
            for i in range(4):
                sc = 4 * g + i
                tile = edge[part, sc // 2, sc % 2].astype(F32)
                picks.append(tile[12:16] if part == 0 else tile[0:4])
            hsend[part, 16 * g : 16 * g + 16, :] = jnp.concatenate(picks, axis=0).astype(BF16)

    many = 2 + jnp.where(az < 15, 1, 0) + jnp.where(az > 0, 1, 0)
    many = many + jnp.where(zc < 3, 1, 0) + jnp.where(zc > 0, 1, 0)
    pl.semaphore_wait(barrier, many)
    for part in range(2):

        @pl.when((az < 15) & (az != 7) if part == 0 else (az > 0) & (az != 8))
        def _():
            h_copy(part).start()

        @pl.when(az == 0 if part == 0 else az == 15)
        def _():
            halo[64 * part : 64 * part + 64, :] = jnp.zeros((64, 2048), BF16)

    pl.when(zc < 3)(lambda: z_copy(zc, 1).start())
    pl.when(zc > 0)(lambda: z_copy(zc, 0).start())
    have(zc)

    build_weights(i0, i1, i2, i3, i4, azw, rgw, flag, eazw, ergw)

    def z_step(d):
        @pl.when(zc + d <= 3)
        def _():
            z_copy(zc + d, 0).wait_recv()
            pl.when(zc > 0)(lambda: z_copy(zc + d, 0).start())
            have(zc + d)

        @pl.when(zc - d >= 0)
        def _():
            z_copy(zc - d, 1).wait_recv()
            pl.when(zc < 3)(lambda: z_copy(zc - d, 1).start())
            have(zc - d)

    def pass_on(d):
        pl.when(zc + d <= 3)(lambda: relay(zc + d))
        pl.when(zc - d >= 0)(lambda: relay(zc - d))

    def pair(first, second):
        first()
        second()

    def far():
        pl.when(az == 7)(lambda: h_copy(0).start())
        pl.when(az == 8)(lambda: h_copy(1).start())

    def step_0():
        z_step(1)
        relay(zc)

    az_steps = [(2, step_0), (4, far)]
    rg_steps = [(10, lambda: z_step(2)), (20, lambda: pass_on(1)), (42, lambda: z_step(3)), (54, lambda: pass_on(2)), (64, lambda: None)]

    azimuth_own(xs, xt_a, xt_b, y, azw, lambda s: x_load(s).wait(), az_steps)
    range_filter(y, z, sums, rgw, flag, edge, et, rg_steps)
    edge_matrices(eazw, ewm, gmat)

    def edges(block):
        @pl.loop(0, 2)
        def _(h):
            for q in range(2):
                edge_cross(block * 4 + 2 * h + q, mt, gmat, ze, esum, flag)

    for g in range(4):
        block = order[g]
        if g == 2:
            pass_on(3)
        if g == 3:
            pl.when(az > 0)(lambda: h_copy(0).wait_recv())
            pl.when(az < 15)(lambda: h_copy(1).wait_recv())
            edge_filter(halo, et, ewm, ye, ze, ergw)
            for e in range(3):
                edges(order[e])
        last(block)

        @pl.loop(0, 2)
        def _(x):
            cross_slab(block * 4 + 2 * x, mt, m32, mp, z, sums, flag)

    edges(order[3])
    finish(sums, esum, out_ref)

    pl.when(az < 15)(lambda: h_copy(0).wait_send())
    pl.when(az > 0)(lambda: h_copy(1).wait_send())
    for block in range(4):
        pl.when((zc < 3) & (block <= zc))(lambda: z_copy(block, 1).wait_send())
        pl.when((zc > 0) & (block >= zc))(lambda: z_copy(block, 0).wait_send())
        for way in range(4):
            x_copy(block, way).wait_send()


def on_device(images, masters, az_shift, rg_shift, az_index, rg_index, segment):
    vmem = pl.BlockSpec(memory_space=pltpu.VMEM)
    dma = pltpu.SemaphoreType.DMA
    return pl.pallas_call(
        kernel,
        out_shape=jax.ShapeDtypeStruct((8, 2, 32, 128), F32),
        in_specs=[pl.BlockSpec(memory_space=pl.ANY)] + [vmem] * 6,
        out_specs=vmem,
        scratch_shapes=[
            pltpu.VMEM((2, 64, 2048), BF16),
            pltpu.VMEM((128, 2048), BF16),
            pltpu.VMEM((16, 4, 128, 128), BF16),
            pltpu.VMEM((8, 2, 128, 2048), BF16),
            pltpu.VMEM((2, 8, 2, 16, 2048), BF16),
            pltpu.VMEM((2, 2048, 128), BF16),
            pltpu.VMEM((2, 2048, 128), BF16),
            pltpu.VMEM((2, 2064 * 8, 128), F32),
            pltpu.VMEM((2, 2048, 8, 128), F32),
            pltpu.VMEM((5, 2048, 128), BF16),
            pltpu.VMEM((2064, 128), F32),
            pltpu.VMEM((2048, 128), F32),
            pltpu.VMEM((4, 256, 128), F32),
            pltpu.VMEM((2, 16, 128), F32),
            pltpu.VMEM((4, 128, 8, 128), F32),
            pltpu.VMEM((4, 128, 128), F32),
            pltpu.VMEM((9, 8, 128), F32),
            pltpu.VMEM((8, 8, 128), F32),
            pltpu.VMEM((3, 8, 128), F32),
            pltpu.VMEM((9, 8, 128), F32),
            pltpu.VMEM((9, 8, 128), F32),
            pltpu.VMEM((640, 256), BF16),
            pltpu.VMEM((256, 256), BF16),
            dma((8,)),
            dma((2,)),
            dma((2,)),
            dma((2,)),
            dma((2, 4)),
            dma((4,)),
            dma((4, 4)),
            dma((4, 4)),
        ],
        compiler_params=pltpu.CompilerParams(
            collective_id=0, has_side_effects=True, vmem_limit_bytes=60 * 2**20
        ),
        name="resample",
    )(images, masters, az_shift, rg_shift, az_index, rg_index, segment)


def solution(mesh):
    return jax.shard_map(
        on_device,
        mesh=mesh,
        in_specs=(
            P("acq", None, "az", None),
            P(None, None, "az", "acq"),
            P("acq", "az"),
            P("acq", "az"),
            P("acq", "az"),
            P("acq", "az"),
            P("acq", "az"),
        ),
        out_specs=P("acq", None, "az", None),
        check_vma=False,
    )
```

```python
import numpy as np

import jax
import jax.numpy as jnp
from jax import lax
from jax.experimental import pallas as pl
from jax.experimental.pallas import tpu as pltpu
from jax.sharding import PartitionSpec as P

MESH = pl.DeviceIdType.MESH
F32, BF16 = jnp.float32, jnp.bfloat16
TAPS, NFRAC = 8, 16
CHUNKS = 4
BOXES = 2


def filter_table():
    x = np.arange(TAPS)[None, :] - 3.0 - np.arange(NFRAC)[:, None] / NFRAC
    taps = np.sinc(x) * (0.5 + 0.5 * np.cos(np.pi * x / 4.0))
    return taps / taps.sum(axis=1, keepdims=True)


def split(value):
    high = value.astype(BF16)
    return high, (value - high.astype(F32)).astype(BF16)


def spread(ints):
    block = lax.broadcasted_iota(jnp.int32, (8, 128), 1) // 16
    out = jnp.zeros((8, 128), F32)
    for b in range(8):
        out = jnp.where(block == b, ints[:, b : b + 1].astype(F32), out)
    return out


def pick(index, column):
    out = jnp.full((8, 128), float(column[0]), F32)
    for f in range(1, NFRAC):
        out = jnp.where(index == float(f), float(column[f]), out)
    return out


def across(ints):
    lane = lax.broadcasted_iota(jnp.int32, (8, 128), 1)
    row = lax.broadcasted_iota(jnp.int32, (8, 128), 0)
    value = ints.astype(F32)
    both = jnp.where(lane % 8 < 4, value[:, 0:1], value[:, 7:8])
    mine = jnp.where(lane // 8 % 8 == row, both, 0.0)
    return jnp.broadcast_to(jnp.sum(mine, axis=0, keepdims=True), (8, 128))


def place(back, taps):
    zero = jnp.zeros((8, 128), F32)
    return [
        jnp.where(back, taps[u] if u < TAPS else zero, taps[u - 1] if u > 0 else zero)
        for u in range(TAPS + 1)
    ]


def build_weights(i0, i1, i2, i3, i4, azw, rgw, flag, eazw, ergw):
    table = filter_table()
    rg_index = spread(i3[...])
    az_index = spread(i2[...])
    centre = pick(rg_index, table[:, 3])
    taps = place(spread(i0[...]) < -0.5, [pick(az_index, table[:, t]) * centre for t in range(TAPS)])
    for u in range(TAPS + 1):
        azw[u] = taps[u]
    for t in range(TAPS):
        rgw[t] = pick(rg_index, table[:, t] / table[:, 3])
    flag[0] = spread(i1[...])
    flag[1] = spread(i4[...])
    flag[2] = across(i4[...])
    rg_index = across(i3[...])
    az_index = across(i2[...])
    taps = place(across(i0[...]) < -0.5, [pick(az_index, table[:, t]) for t in range(TAPS)])
    more = place(across(i1[...]) < -0.5, [pick(rg_index, table[:, t]) for t in range(TAPS)])
    for u in range(TAPS + 1):
        eazw[u] = taps[u]
        ergw[u] = more[u]


def azimuth_own(xs, xt_a, xt_b, y, azw, wait, steps):
    rows = lax.broadcasted_iota(jnp.int32, (128, 128), 0)
    lanes = lax.broadcasted_iota(jnp.int32, (128, 128), 1)
    for c in range(2):
        y[c, 0:64, :] = jnp.zeros((64, 128), F32)
        y[c, 8 * 2056 : 8 * 2064, :] = jnp.zeros((64, 128), F32)

    def turn(s, dst):
        for c in range(2):
            for k in range(16):
                part = slice(k * 128, (k + 1) * 128)
                dst[c, part, :] = xs[s, c, :, part].T

    def half(s, cur, nxt):
        pl.when(s < 7)(lambda: wait(s + 1))
        offset = rows - lanes
        own = jnp.zeros((128, 128), F32)
        for u in range(9):
            own = jnp.where(offset == u - 4, azw[u, pl.ds(s, 1), :], own)
        matrix = jnp.concatenate(split(own), axis=0)
        for c in range(2):
            for k in range(CHUNKS):
                n = 2048 // CHUNKS
                lhs = cur[c, k * n : (k + 1) * n, :]
                y[c, pl.ds(64 + 8 * n * k + s, n, stride=8), :] = jnp.dot(
                    jnp.concatenate([lhs, lhs], axis=1), matrix, preferred_element_type=F32
                )
        turn(jnp.minimum(s + 1, 7), nxt)

    wait(0)
    turn(0, xt_a)

    start = 0
    for stop, step in steps:

        @pl.loop(start, stop)
        def _(p):
            half(2 * p, xt_a, xt_b)
            half(2 * p + 1, xt_b, xt_a)

        step()
        start = stop


def range_filter(y, z, sums, rgw, flag, edge, et, steps):
    w = [rgw[t] for t in range(TAPS)]

    def boxes(i):
        back = flag[0] < -0.5
        base = pl.multiple_of(i * (128 * BOXES), 128)
        cols = pl.ds(pl.multiple_of(i % 16 * 128, 128), 128)
        block = edge[i // 32, pl.ds(i // 16 % 2 * 4, 4), :, :, cols].reshape(128, 128)
        et[i // 16, cols, :] = block.T
        psum = [None] * BOXES
        for c in range(2):

            def load(q):
                return y[c, pl.ds(base + 64 + 8 * q, 8), :]

            before, win = load(-4), []
            for q in range(-3, 16 * BOXES + 4):
                row = load(q)
                win = (win + [jnp.where(back, before, row)])[-8:]
                before = row
                k = q - 4
                if k < 0:
                    continue
                acc = win[3]
                for t in (0, 1, 2, 4, 5, 6, 7):
                    acc = acc + w[t] * win[t]
                z[c, 16 * BOXES * i + k] = acc
                sq = acc * acc
                b = k // 16
                psum[b] = sq if psum[b] is None else psum[b] + sq
        for b in range(BOXES):
            sums[2, BOXES * i + b] = psum[b]

    start = 0
    for stop, step in steps:
        pl.loop(start, stop)(boxes)
        step()
        start = stop


def edge_line(lane):
    return jnp.where(lane % 8 < 4, lane % 8, 120 + lane % 8)


def edge_matrices(eazw, ewm, gmat):
    row = lax.broadcasted_iota(jnp.int32, (128, 128), 0)
    lane = lax.broadcasted_iota(jnp.int32, (128, 128), 1)
    image = lane // 8 % 8 * 2 + lane // 64
    at = edge_line(lane)

    def banded(line, owner, where):
        offset = jnp.where(owner == image, line - at, 1000)
        out = jnp.zeros((128, 128), F32)
        for u in range(9):
            out = jnp.where(offset == u - 4, eazw[u, 0:1, :], out)
        high, low = split(out)
        ewm[where, 0:128] = high
        ewm[where, 128:256] = low

    for q in range(4):
        banded(row % 16 + (112 if q < 2 else 0), q % 2 * 8 + row // 16, slice(128 * q, 128 * q + 128))
    banded(jnp.where(row < 64, row % 4 - 4, 128 + row % 4), row % 64 // 4, slice(512, 640))
    hit = (row == at).astype(F32)
    left = lane < 64
    zero = jnp.zeros((128, 128), F32)
    gmat[0:128, 0:128] = jnp.where(left, hit, zero).astype(BF16)
    gmat[128:256, 0:128] = jnp.where(left, zero, hit).astype(BF16)
    gmat[0:128, 128:256] = jnp.where(left, zero, hit).astype(BF16)
    gmat[128:256, 128:256] = jnp.where(left, -hit, zero).astype(BF16)


def edge_filter(halo, et, ewm, ye, ze, ergw):
    @pl.loop(0, 4)
    def _(k):
        for i in range(4):
            cols = pl.ds(pl.multiple_of(k * 512 + i * 128, 128), 128)
            et[4, cols, :] = halo[:, cols].T

    for k in range(2):
        part = slice(1024 * k, 1024 * k + 1024)
        lhs = jnp.concatenate([et[q, part, :] for q in range(5)], axis=1)
        res = jnp.dot(lhs, ewm[...], preferred_element_type=F32)
        ye[8 + 1024 * k : 8 + 1024 * k + 1024, :] = res[:, 0:128] + res[:, 128:256]
    ye[0:8, :] = jnp.zeros((8, 128), F32)
    ye[2056:2064, :] = jnp.zeros((8, 128), F32)

    @pl.loop(0, 32)
    def _(k):
        base = pl.multiple_of(k * 64, 64)
        acc = ergw[0, 0:1, :] * ye[pl.ds(base + 4, 64), :]
        for u in range(1, 9):
            acc = acc + ergw[u, 0:1, :] * ye[pl.ds(base + 4 + u, 64), :]
        ze[pl.ds(base, 64), :] = acc


def edge_cross(j, mt, gmat, ze, esum, flag):
    sel = flag[2, 0:1, :] > 0.5
    m = [
        jnp.dot(
            jnp.concatenate([mt[j, 2 * q], mt[j, 2 * q + 1]], axis=1),
            gmat[...],
            preferred_element_type=F32,
        )
        for q in range(2)
    ]
    one = jnp.where(sel, m[1][:, 0:128], m[0][:, 0:128])
    two = jnp.where(sel, m[1][:, 128:256], m[0][:, 128:256])
    v = ze[pl.ds(pl.multiple_of(j * 128, 128), 128), :]
    for q, product in enumerate((v * one, v * two, v * v, one * one)):
        esum[q, pl.ds(pl.multiple_of(j * 8, 8), 8), :] = jnp.sum(product.reshape(8, 16, 128), axis=1)


def cross_slab(j, mt, m32, mp, z, sums, flag):
    sel = flag[1] > 0.5

    def row(ref, r):
        return jnp.broadcast_to(ref[pl.ds(r, 1), :], (8, 128))

    for q in range(2):
        rows = slice(128 * q, 128 * q + 128)
        for p in range(4):
            m32[p, rows] = mt[j + q, p].astype(F32)
        for m in range(2):
            t = m32[2 * m, rows] * m32[2 * m, rows] + m32[2 * m + 1, rows] * m32[2 * m + 1, rows]
            mp[m, 8 * q : 8 * q + 8] = jnp.sum(t.reshape(8, 16, 128), axis=1)

    @pl.loop(0, 8)
    def _(h):
        for i in (2 * h, 2 * h + 1):
            box = j * 8 + i
            sums[3, box] = jnp.where(sel, row(mp.at[1], i), row(mp.at[0], i))
            re = im = None
            for k in range(16):
                r = 16 * i + k
                a = z[0, box * 16 + k]
                b = z[1, box * 16 + k]
                c = jnp.where(sel, row(m32.at[2], r), row(m32.at[0], r))
                d = jnp.where(sel, row(m32.at[3], r), row(m32.at[1], r))
                t = a * c + b * d
                q = b * c - a * d
                re = t if re is None else re + t
                im = q if im is None else im + q
            sums[0, box] = re
            sums[1, box] = im


def finish(sums, esum, out_ref):
    dn = (((1,), (1,)), ((), ()))

    def folded(e, value):
        high, low = split(value)
        return lax.dot_general(e, high, dn, preferred_element_type=F32) + lax.dot_general(
            e, low, dn, preferred_element_type=F32
        )

    row = lax.broadcasted_iota(jnp.int32, (32, 128), 0)
    lane = lax.broadcasted_iota(jnp.int32, (32, 128), 1)
    lines = (row == lane // 4).astype(BF16)

    @pl.loop(0, 2)
    def _(p):
        for s in (4 * p, 4 * p + 1, 4 * p + 2, 4 * p + 3):
            g = [
                folded(lines, sums.at[q].reshape(1024, 128)[pl.ds(s, 128, stride=8), :])
                for q in range(4)
            ]
            inverse = 1.0 / jnp.sqrt(g[2] * g[3] + 1e-6)
            out_ref[s, 0] = g[0] * inverse
            out_ref[s, 1] = g[1] * inverse

    ends = ((row // 2 == lane // 8 % 8) & (row % 2 == lane % 8 // 4)).astype(BF16)
    g = [folded(ends, esum[q]) for q in range(4)]
    inverse = 1.0 / jnp.sqrt(g[2] * g[3] + 1e-6)
    for part in range(2):
        value = g[part] * inverse
        for s in range(8):
            out_ref[s, part, 0:1, :] = value[2 * s : 2 * s + 1, :]
            out_ref[s, part, 31:32, :] = value[2 * s + 1 : 2 * s + 2, :]

def kernel(
    x_hbm, m_ref, i0, i1, i2, i3, i4, out_ref,
    hsend, halo, mt,
    xs, edge, xt_a, xt_b, y, z, et, ye, ze, m32, mp, sums, esum, azw, rgw, flag, eazw, ergw, ewm, gmat,
    x_sem, e_sem, hs_sem, hr_sem, zs_sem, zr_sem, xs_sem, xr_sem,
):
    acq = lax.axis_index("acq")
    az = lax.axis_index("az")
    zc, xc = acq // 4, acq % 4
    right, left = zc * 4 + (xc + 1) % 4, zc * 4 + (xc + 3) % 4
    inner = (zc == 1) | (zc == 2)
    low = zc < 2
    order = [
        zc,
        jnp.where(low, zc + 1, zc - 1),
        jnp.where(inner, jnp.where(low, 0, 3), jnp.where(low, 2, 1)),
        jnp.where(low, 3, 0),
    ]

    def edge_copy(part):
        rows = pl.ds(112 * (1 - part), 16)
        return pltpu.make_async_copy(x_hbm.at[:, :, rows, :], edge.at[part], e_sem.at[part])

    def x_load(s):
        return pltpu.make_async_copy(x_hbm.at[s], xs.at[s], x_sem.at[s])

    for part in range(2):
        edge_copy(part).start()
    for s in range(8):
        x_load(s).start()

    barrier = pltpu.get_barrier_semaphore()

    def greet(a, b):
        pl.semaphore_signal(barrier, inc=1, device_id=(a, b), device_id_type=MESH)

    greet(right, az)
    greet(left, az)
    pl.when(zc < 3)(lambda: greet(acq + 4, az))
    pl.when(zc > 0)(lambda: greet(acq - 4, az))
    pl.when(az < 15)(lambda: greet(acq, az + 1))
    pl.when(az > 0)(lambda: greet(acq, az - 1))
    for p in range(4):
        mt[acq, p] = m_ref[p // 2, p % 2].T

    def z_copy(block, up):
        ref = mt.at[block * 4 + xc]
        return pltpu.make_async_remote_copy(
            src_ref=ref, dst_ref=ref,
            send_sem=zs_sem.at[up, block], recv_sem=zr_sem.at[block],
            device_id=(acq + 4 if up else acq - 4, az), device_id_type=MESH,
        )

    def x_copy(block, way):
        origin = [xc, xc, (xc + 3) % 4, (xc + 1) % 4][way]
        part = [slice(0, 4), slice(0, 4), slice(0, 2), slice(2, 4)][way]
        ref = mt.at[block * 4 + origin, part]
        return pltpu.make_async_remote_copy(
            src_ref=ref, dst_ref=ref,
            send_sem=xs_sem.at[way, block], recv_sem=xr_sem.at[way, block],
            device_id=(right if way % 2 == 0 else left, az), device_id_type=MESH,
        )

    def h_copy(part):
        return pltpu.make_async_remote_copy(
            src_ref=hsend.at[part], dst_ref=halo.at[pl.ds(64 * part, 64), :],
            send_sem=hs_sem.at[part], recv_sem=hr_sem.at[part],
            device_id=(acq, az + 1 if part == 0 else az - 1), device_id_type=MESH,
        )

    def have(block):
        x_copy(block, 0).start()
        x_copy(block, 1).start()

    def relay(block):
        x_copy(block, 0).wait_recv()
        x_copy(block, 2).start()
        x_copy(block, 1).wait_recv()
        x_copy(block, 3).start()

    def last(block):
        x_copy(block, 2).wait_recv()
        x_copy(block, 3).wait_recv()

    for part in range(2):
        edge_copy(part).wait()
        for g in range(4):
            picks = []
            for i in range(4):
                sc = 4 * g + i
                tile = edge[part, sc // 2, sc % 2].astype(F32)
                picks.append(tile[12:16] if part == 0 else tile[0:4])
            hsend[part, 16 * g : 16 * g + 16, :] = jnp.concatenate(picks, axis=0).astype(BF16)

    build_weights(i0, i1, i2, i3, i4, azw, rgw, flag, eazw, ergw)
    edge_matrices(eazw, ewm, gmat)

    many = 2 + jnp.where(az < 15, 1, 0) + jnp.where(az > 0, 1, 0)
    many = many + jnp.where(zc < 3, 1, 0) + jnp.where(zc > 0, 1, 0)
    pl.semaphore_wait(barrier, many)
    for part in range(2):

        @pl.when((az < 15) & (az != 7) if part == 0 else (az > 0) & (az != 8))
        def _():
            h_copy(part).start()

        @pl.when(az == 0 if part == 0 else az == 15)
        def _():
            halo[64 * part : 64 * part + 64, :] = jnp.zeros((64, 2048), BF16)

    pl.when(zc < 3)(lambda: z_copy(zc, 1).start())
    pl.when(zc > 0)(lambda: z_copy(zc, 0).start())
    have(zc)

    def z_step(d):
        @pl.when(zc + d <= 3)
        def _():
            z_copy(zc + d, 0).wait_recv()
            pl.when(zc > 0)(lambda: z_copy(zc + d, 0).start())
            have(zc + d)

        @pl.when(zc - d >= 0)
        def _():
            z_copy(zc - d, 1).wait_recv()
            pl.when(zc < 3)(lambda: z_copy(zc - d, 1).start())
            have(zc - d)

    def pass_on(d):
        pl.when(zc + d <= 3)(lambda: relay(zc + d))
        pl.when(zc - d >= 0)(lambda: relay(zc - d))

    def pair(first, second):
        first()
        second()

    def far():
        pl.when(az == 7)(lambda: h_copy(0).start())
        pl.when(az == 8)(lambda: h_copy(1).start())

    def step_0():
        z_step(1)
        relay(zc)

    az_steps = [(2, step_0), (4, far)]
    rg_steps = [(10, lambda: z_step(2)), (20, lambda: pass_on(1)), (42, lambda: z_step(3)), (54, lambda: pass_on(2)), (64, lambda: None)]

    azimuth_own(xs, xt_a, xt_b, y, azw, lambda s: x_load(s).wait(), az_steps)
    range_filter(y, z, sums, rgw, flag, edge, et, rg_steps)

    def edges(block):
        @pl.loop(0, 2)
        def _(h):
            for q in range(2):
                edge_cross(block * 4 + 2 * h + q, mt, gmat, ze, esum, flag)

    for g in range(4):
        block = order[g]
        if g == 2:
            pass_on(3)
        if g == 3:
            pl.when(az > 0)(lambda: h_copy(0).wait_recv())
            pl.when(az < 15)(lambda: h_copy(1).wait_recv())
            edge_filter(halo, et, ewm, ye, ze, ergw)
            for e in range(3):
                edges(order[e])
        last(block)

        @pl.loop(0, 2)
        def _(x):
            cross_slab(block * 4 + 2 * x, mt, m32, mp, z, sums, flag)

    edges(order[3])
    finish(sums, esum, out_ref)

    pl.when(az < 15)(lambda: h_copy(0).wait_send())
    pl.when(az > 0)(lambda: h_copy(1).wait_send())
    for block in range(4):
        pl.when((zc < 3) & (block <= zc))(lambda: z_copy(block, 1).wait_send())
        pl.when((zc > 0) & (block >= zc))(lambda: z_copy(block, 0).wait_send())
        for way in range(4):
            x_copy(block, way).wait_send()


def on_device(images, masters, az_shift, rg_shift, az_index, rg_index, segment):
    vmem = pl.BlockSpec(memory_space=pltpu.VMEM)
    dma = pltpu.SemaphoreType.DMA
    return pl.pallas_call(
        kernel,
        out_shape=jax.ShapeDtypeStruct((8, 2, 32, 128), F32),
        in_specs=[pl.BlockSpec(memory_space=pl.ANY)] + [vmem] * 6,
        out_specs=vmem,
        scratch_shapes=[
            pltpu.VMEM((2, 64, 2048), BF16),
            pltpu.VMEM((128, 2048), BF16),
            pltpu.VMEM((16, 4, 128, 128), BF16),
            pltpu.VMEM((8, 2, 128, 2048), BF16),
            pltpu.VMEM((2, 8, 2, 16, 2048), BF16),
            pltpu.VMEM((2, 2048, 128), BF16),
            pltpu.VMEM((2, 2048, 128), BF16),
            pltpu.VMEM((2, 2064 * 8, 128), F32),
            pltpu.VMEM((2, 2048, 8, 128), F32),
            pltpu.VMEM((5, 2048, 128), BF16),
            pltpu.VMEM((2064, 128), F32),
            pltpu.VMEM((2048, 128), F32),
            pltpu.VMEM((4, 256, 128), F32),
            pltpu.VMEM((2, 16, 128), F32),
            pltpu.VMEM((4, 128, 8, 128), F32),
            pltpu.VMEM((4, 128, 128), F32),
            pltpu.VMEM((9, 8, 128), F32),
            pltpu.VMEM((8, 8, 128), F32),
            pltpu.VMEM((3, 8, 128), F32),
            pltpu.VMEM((9, 8, 128), F32),
            pltpu.VMEM((9, 8, 128), F32),
            pltpu.VMEM((640, 256), BF16),
            pltpu.VMEM((256, 256), BF16),
            dma((8,)),
            dma((2,)),
            dma((2,)),
            dma((2,)),
            dma((2, 4)),
            dma((4,)),
            dma((4, 4)),
            dma((4, 4)),
        ],
        compiler_params=pltpu.CompilerParams(
            collective_id=0, has_side_effects=True, vmem_limit_bytes=60 * 2**20
        ),
        name="resample",
    )(images, masters, az_shift, rg_shift, az_index, rg_index, segment)


def solution(mesh):
    return jax.shard_map(
        on_device,
        mesh=mesh,
        in_specs=(
            P("acq", None, "az", None),
            P(None, None, "az", "acq"),
            P("acq", "az"),
            P("acq", "az"),
            P("acq", "az"),
            P("acq", "az"),
            P("acq", "az"),
        ),
        out_specs=P("acq", None, "az", None),
        check_vma=False,
    )
```
